32 devices in a mesh: expert: 2 (over x), tensor: 16 (over z, y, core).
Axes of the slice: x: 2, y: 2, z: 4, core: 2. Of those that a mesh axis runs over, the one named last changes fastest.
Arguments:
- tokens: bfloat16 [128, 6144], P(('expert', 'tensor')), may hold values from -6 to 6
- gate_weights: bfloat16 [128, 2], P(('expert', 'tensor')), may hold values from 0.19921875 to 1
- expert_ids: int32 [128, 2], P(('expert', 'tensor')), may hold values from 0 to 3, all different within a row; in each aligned block of 128 rows (0 to 127, 128 to 255, ...) at most 96 rows name the same one
- w_gate: bfloat16 [4, 6144, 16384], P('expert', None, 'tensor'), may hold values from -0.078125 to 0.078125
- w_up: bfloat16 [4, 6144, 16384], P('expert', None, 'tensor'), may hold values from -0.078125 to 0.078125
- w_down: bfloat16 [4, 16384, 6144], P('expert', 'tensor'), may hold values from -0.046875 to 0.046875
Outputs:
- mixed: bfloat16 [128, 6144], P(('expert', 'tensor'))
The draws below stay inside these ranges and needn't reach their ends.
Inputs may be any that keep to these rules, and one draw needn't show every extreme that they name: `expert_ids`: the 2 ids of a token differ; every expert is named by at most 96 tokens, a bound that some block reaches.
All inputs are finite; a program needn't handle non-finite values.
Results may differ from the reference program's by a relative error of at most 0.0049.
Values may be sent and summed in bfloat16 or wider, within the bound.
No kernel may reach another device: no remote copies, remote signals or barrier semaphores. Data moves between devices by JAX's collectives and lax.ppermute only.
A program may use at most 192 MiB of HBM per device.

```python
import math
import jax
import jax.numpy as jnp
import numpy as np

D = 6144
FF = 16384
TOP = 2
EXPERTS = 4
TOKENS = 128
CAP = 96


def block_levels(own_key, shape, pieces, low, high):
    def one(dim, parts):
        heights = jax.random.uniform(jax.random.fold_in(jax.random.fold_in(own_key, 6), dim), (parts,), jnp.float32, low / len(pieces), high / len(pieces))
        return jnp.repeat(jnp.exp(heights), shape[dim] // parts).reshape((-1,) + (1,) * (len(shape) - dim - 1))

    factor_of = one(*pieces[0])
    for cut in pieces[1:]:
        factor_of = factor_of * one(*cut)
    return factor_of


def shared_out(rng, own, number, rows, count, top, bound, slope):
    order = jax.random.permutation(rng, count)
    heavy_load, ordinary = portions_of(count, rows * top, bound, slope, True), portions_of(count, rows * top, bound, slope, False)
    places = jnp.arange(count)

    def named(sizes, turn):
        used = int((sizes > 0).sum())
        fixed = max(1, used // 4)
        shifted = fixed + (places - fixed + turn * (used - fixed)) % max(1, count - fixed)
        return jnp.zeros((count,), jnp.int32).at[order[jnp.where(places < fixed, places, shifted)]].set(jnp.asarray(sizes, jnp.int32))

    sizes = jnp.where(number % 4 == 0, named(heavy_load, number // 4), named(ordinary, number - number // 4 - 1))
    mixed = jax.random.permutation(jax.random.fold_in(own, 3), count)
    donor, sink = mixed[0:count // 2 * 2:2], mixed[1:count // 2 * 2:2]
    margin = jnp.minimum(sizes[donor] - 1, bound - sizes[sink]) // 2
    margin = jnp.where((donor == order[0]) | (sink == order[0]) | (sizes[sink] == 0), 0, jnp.maximum(margin, 0))
    shifted = jax.random.randint(jax.random.fold_in(own, 4), (count // 2,), 0, 1 << 20) % (margin + 1)
    sizes = sizes.at[donor].add(-shifted).at[sink].add(shifted)
    labels = jnp.searchsorted(jnp.cumsum(sizes), jnp.arange(rows * top), side="right").astype(jnp.int32)
    listing = labels.reshape(top, rows).T
    listing = listing[jax.random.permutation(jax.random.fold_in(own, 1), rows)]
    turn = jax.random.randint(jax.random.fold_in(own, 2), (rows, 1), 0, top)
    return jnp.take_along_axis(listing, (jnp.arange(top)[None, :] + turn) % top, axis=1)


def portions_of(number_of, total, limit, slope, full):
    loads = [(1 << 20) // math.isqrt(grade ** slope) + 1 for grade in range(1, number_of + 1)]
    largest = limit if full else min(limit, max(-(-total // number_of), total * loads[0] // sum(loads)))
    least = 1 if total - largest >= number_of - 1 else 0
    counts, surplus = [largest] + [least] * (number_of - 1), total - largest - least * (number_of - 1)
    while surplus > 0:
        movable = [i for i in range(1, number_of) if counts[i] < largest] or [i for i in range(1, number_of) if counts[i] < limit]
        pool, remaining = sum([loads[i] for i in movable]), surplus
        for i in movable:
            addition = min(limit - counts[i], max(1, remaining * loads[i] // pool), surplus)
            counts[i] = counts[i] + addition
            surplus = surplus - addition
    return np.array(counts)


def noise(rng, dims, scale, reach, split=(), kind=jnp.bfloat16):
    loudness = block_levels(rng, dims, split, -0.22, 0.18) if split else 1.0
    array = jax.random.normal(rng, dims, jnp.float32) * scale * loudness
    return jnp.minimum(jnp.maximum(array, -reach), reach).astype(kind)


def setup_inputs(seed: int = 0) -> dict:
    arg_keys = jax.random.split(jax.random.key(seed), 7)
    tokens = noise(arg_keys[0], (TOKENS, D), 1.0, 6.0, ((0, 32),))
    gate_weights = jnp.clip(0.19921875 + 0.80078125 * jax.random.uniform(arg_keys[1], (TOKENS, TOP), jnp.float32) ** block_levels(arg_keys[1], (TOKENS, TOP), ((0, 32),), -0.2, 0.2), 0.19921875, 1.0).astype(jnp.bfloat16)
    expert_ids_keys = jax.random.split(jax.random.fold_in(arg_keys[2], 1), TOKENS // TOKENS)
    expert_ids_turns = jax.random.permutation(jax.random.fold_in(arg_keys[2], 3), TOKENS // TOKENS)
    expert_ids = jax.vmap(lambda own, number: shared_out(jax.random.fold_in(arg_keys[2], 2), own, number, TOKENS, EXPERTS, TOP, CAP, 2))(expert_ids_keys, expert_ids_turns).reshape((TOKENS, TOP))
    w_gate = noise(arg_keys[3], (EXPERTS, D, FF), D ** -0.5, 0.078125, ((0, 2), (2, 16)))
    w_up = noise(arg_keys[4], (EXPERTS, D, FF), D ** -0.5, 0.078125, ((0, 2), (2, 16)))
    w_down = noise(arg_keys[5], (EXPERTS, FF, D), FF ** -0.5, 0.046875, ((0, 2), (1, 16)))
    return {"tokens": tokens, "gate_weights": gate_weights, "expert_ids": expert_ids, "w_gate": w_gate, "w_up": w_up, "w_down": w_down}


def routing_lists(expert_ids, gate_weights, expert, capacity):
    matches = expert_ids == expert
    chosen = jnp.any(matches, axis=1)
    weight = jnp.sum(jnp.where(matches, gate_weights.astype(jnp.float32), jnp.float32(0.0)), axis=1)
    ranking = jnp.cumsum(chosen.astype(jnp.int32)) - 1
    target = jnp.where(chosen, ranking, capacity).astype(jnp.int32)
    token_count = expert_ids.shape[0]
    slot_tok = jnp.full((capacity,), token_count, jnp.int32).at[target].set(
        jnp.arange(token_count, dtype=jnp.int32), mode="drop")
    slot_gate = jnp.zeros((capacity,), jnp.float32).at[target].set(weight, mode="drop")
    return slot_tok, slot_gate


def reference(tokens, gate_weights, expert_ids, w_gate, w_up, w_down):
    summed = jnp.zeros((TOKENS, D), jnp.float32)
    for expert in range(EXPERTS):
        slot_tok, slot_gate = routing_lists(expert_ids, gate_weights, expert, CAP)
        slot_rows = tokens[jnp.minimum(slot_tok, TOKENS - 1)]
        gate_proj = jnp.dot(slot_rows, w_gate[expert], preferred_element_type=jnp.float32)
        up_proj = jnp.dot(slot_rows, w_up[expert], preferred_element_type=jnp.float32)
        hidden = (jax.nn.silu(gate_proj) * up_proj).astype(jnp.bfloat16)
        expert_out = jnp.dot(hidden, w_down[expert], preferred_element_type=jnp.float32)
        summed = summed.at[slot_tok].add(expert_out * slot_gate[:, None], mode="drop")
    return summed.astype(jnp.bfloat16)
```

```python
import functools
import jax
import jax.numpy as jnp
from jax import lax
from jax.experimental import pallas as pl
from jax.experimental.pallas import tpu as pltpu
from jax.sharding import PartitionSpec as P

LANES = 128
BOTH = ("expert", "tensor")
VMEM = pl.BlockSpec(memory_space=pltpu.VMEM)
HBM = pl.BlockSpec(memory_space=pltpu.HBM)
MIB = 1 << 20
RING = 6


def exchange(x, ke, kt):
    ne, nt = lax.axis_size("expert"), lax.axis_size("tensor")
    pairs = [(e * nt + t, (e ^ ke) * nt + (t ^ kt)) for e in range(ne) for t in range(nt)]
    return lax.ppermute(x, BOTH, pairs)


def near_offsets():
    return [(e, y) for e in range(lax.axis_size("expert")) for y in (0, 2)][1:]


def far_offsets():
    return [(0, 4 * k) for k in range(1, lax.axis_size("tensor") // 4)]


def in_vmem(x):
    return pltpu.with_memory_space_constraint(x, pltpu.VMEM)


def unit_of(ref, spot):
    kind, e, half, h = spot
    return ref.at[e, :, pl.ds(half * h, h)] if kind == 2 else ref.at[e, pl.ds(half * h, h), :]


def stage(compute, weights, loads, deps, ins, outs, scratch, flops, limit):
    n_load, n_in = len(loads), len(ins)
    kinds = sorted({spot[0] for spot in loads})
    used = [weights[k] for k in kinds]
    e_count, d, f = weights[0].shape
    shapes = [(f, spot[3]) if spot[0] == 2 else (spot[3], f) for spot in loads]

    def kernel(*refs):
        refs = list(refs)
        hbm = {k: refs.pop(0) for k in kinds}
        del refs[: len(deps)]
        in_refs = [refs.pop(0) for _ in range(n_in)]
        unit_refs = [refs.pop(0) for _ in range(n_load)]
        token_ref = refs.pop(0)
        out_refs = [refs.pop(0) for _ in outs]
        sems = refs.pop() if n_load else None
        copies = [
            pltpu.make_async_copy(unit_of(hbm[spot[0]], spot), unit_refs[i], sems.at[i])
            for i, spot in enumerate(loads)
        ]
        for copy in copies:
            copy.start()
        token_ref[...] = jnp.zeros_like(token_ref)
        if compute is not None:
            compute(in_refs, out_refs, refs)
        for copy in copies:
            copy.wait()

    size = sum(2 * a * b for a, b in shapes)
    results = pl.pallas_call(
        kernel,
        in_specs=[HBM] * len(used) + [pl.BlockSpec(memory_space=pl.ANY)] * len(deps) + [VMEM] * n_in,
        out_specs=[VMEM] * (n_load + 1 + len(outs)),
        out_shape=[pltpu.VMEM(s, jnp.bfloat16) for s in shapes]
        + [pltpu.VMEM((8, LANES), jnp.float32)]
        + [pltpu.VMEM(s, t) for s, t in outs],
        scratch_shapes=list(scratch) + ([pltpu.SemaphoreType.DMA((n_load,))] if n_load else []),
        compiler_params=pltpu.CompilerParams(vmem_limit_bytes=limit),
        cost_estimate=pl.CostEstimate(flops=flops, bytes_accessed=size, transcendentals=0),
    )(*[pltpu.with_memory_space_constraint(w, pltpu.HBM) for w in used], *deps, *[in_vmem(x) for x in ins])
    return list(results[:n_load]), results[n_load], list(results[n_load + 1 :])


def columns(count, step, body):
    @pl.loop(0, count // step)
    def _(i):
        body(pl.ds(pl.multiple_of(i * step, step), step))


def dot(a, b):
    return jnp.dot(a, b, preferred_element_type=jnp.float32)


def shards(tokens, gate_weights, expert_ids, w_gate, w_up, w_down):
    weights = (w_gate, w_up, w_down)
    e_count, d, f = w_gate.shape
    ne, nt = lax.axis_size("expert"), lax.axis_size("tensor")
    own = tokens.shape[0]
    total = own * ne * nt
    half = d // 2
    fb = min(256, f)
    rows = own * (nt // 4)

    experts = lax.broadcasted_iota(jnp.int32, (1, LANES), 1)
    gates = sum(
        jnp.where(expert_ids[:, i : i + 1] == experts, gate_weights[:, i : i + 1], jnp.bfloat16(0))
        for i in range(expert_ids.shape[1])
    )
    packed = jnp.concatenate([gates, tokens], axis=1)

    def load_only(loads, *deps):
        units, token, _ = stage(None, weights, loads, deps, [], [], [], 0, 2 * MIB)
        return units, token

    last = e_count - 1
    resident = [(k, e, h, half) for e in range(last) for k in (0, 1) for h in (0, 1)]
    resident += [(0, last, 0, half), (1, last, 0, half)]
    cut = len(resident) // 2
    far = [exchange(packed, *k) for k in far_offsets()]
    units, token = load_only(resident[:cut], packed)
    block = jnp.concatenate([packed] + far, axis=0)
    block, token = lax.optimization_barrier((block, token))
    pieces = [block] + [exchange(block, *k) for k in near_offsets()]
    more, token = load_only(resident[cut:], block, token)
    pieces[-1], token = lax.optimization_barrier((pieces[-1], token))
    units = units + more
    pieces = pieces + [exchange(p, 0, 1) for p in pieces]

    chunk = 1024
    n_k, n_d = half // chunk, d // chunk
    stream = [(k, j) for j in range(n_k) for k in (0, 1)]
    stream += [(2 + e, j) for j in range(n_d) for e in range(e_count)]
    slots = RING

    def kernel(*refs):
        refs = list(refs)
        wg, wu, wd = refs[:3]
        del refs[:4]
        xrefs = [refs.pop(0) for _ in pieces]
        held = {spot[:3]: refs.pop(0) for spot in resident}
        sends = [refs.pop(0) for _ in range(2)]
        keeps = [refs.pop(0) for _ in range(2)]
        xs, gate_ref, g_ref, u_ref, h_ref, ring, sems = refs

        def slot(i):
            kind, j = stream[i]
            view = ring.at[i % slots]
            return view.at[:chunk, :f] if kind < 2 else view.at[:f, :chunk]

        def copy(i):
            kind, j = stream[i]
            if kind < 2:
                src = (wg, wu)[kind].at[last, pl.ds(half + j * chunk, chunk), :]
            else:
                src = wd.at[kind - 2, :, pl.ds(j * chunk, chunk)]
            return pltpu.make_async_copy(src, slot(i), sems.at[i % slots])

        for i in range(slots):
            copy(i).start()

        me = lax.axis_index("expert")
        for i, ref in enumerate(xrefs):
            r = slice(i * rows, (i + 1) * rows)
            xs[r, :] = ref[:, LANES:]
            meta = ref[:, :LANES].astype(jnp.float32)
            lane = lax.broadcasted_iota(jnp.int32, meta.shape, 1)
            for e in range(e_count):
                col = jnp.sum(jnp.where(lane == me * e_count + e, meta, 0.0), axis=1, keepdims=True)
                gate_ref[e, r, :] = jnp.broadcast_to(col, meta.shape)

        def hide(e, c, g, u):
            h_ref[e, :, c] = (g / (1.0 + jnp.exp(-g)) * u).astype(jnp.bfloat16)

        def begin(c):
            g_ref[:, c] = dot(xs[:, :half], held[0, last, 0][:, c])
            u_ref[:, c] = dot(xs[:, :half], held[1, last, 0][:, c])

        columns(f, fb, begin)
        for j in range(n_k):
            k = slice(half + j * chunk, half + (j + 1) * chunk)
            sg, su = slot(2 * j), slot(2 * j + 1)
            copy(2 * j).wait()
            copy(2 * j + 1).wait()

            def add(c):
                g = g_ref[:, c] + dot(xs[:, k], sg[:, c])
                u = u_ref[:, c] + dot(xs[:, k], su[:, c])
                if j < n_k - 1:
                    g_ref[:, c] = g
                    u_ref[:, c] = u
                else:
                    hide(last, c, g, u)

            columns(f, fb, add)
            for i in (2 * j, 2 * j + 1):
                if i + slots < len(stream):
                    copy(i + slots).start()
        for e in range(last):

            def whole(c):
                g = dot(xs[:, :half], held[0, e, 0][:, c]) + dot(xs[:, half:], held[0, e, 1][:, c])
                u = dot(xs[:, :half], held[1, e, 0][:, c]) + dot(xs[:, half:], held[1, e, 1][:, c])
                hide(e, c, g, u)

            columns(f, fb, whole)
        for j in range(n_d):
            at = [2 * n_k + j * e_count + e for e in range(e_count)]
            views = [slot(i) for i in at]
            for i in at:
                copy(i).wait()
            side, start = divmod(j * chunk, half)

            def out(c):
                s = sum(dot(h_ref[e], views[e][:, c]) * gate_ref[e, :, 0:1] for e in range(e_count))
                to = pl.ds(pl.multiple_of(c.start + start, 256), 256)
                keeps[side][:, to] = s[: total // 2]
                sends[side][:, to] = s[total // 2 :].astype(jnp.bfloat16)

            columns(chunk, 256, out)
            for i in at:
                if i + slots < len(stream):
                    copy(i + slots).start()

    side_len = max(chunk, f)
    scratch = 2 * total * d + 4 * e_count * total * LANES + 8 * total * f + 2 * e_count * total * f
    scratch += 2 * slots * side_len * side_len
    ins = pieces + units
    results = pl.pallas_call(
        kernel,
        in_specs=[HBM] * 3 + [pl.BlockSpec(memory_space=pl.ANY)] + [VMEM] * len(ins),
        out_specs=[VMEM] * 4,
        out_shape=[pltpu.VMEM((total // 2, half), jnp.bfloat16)] * 2
        + [pltpu.VMEM((total // 2, half), jnp.float32)] * 2,
        scratch_shapes=[
            pltpu.VMEM((total, d), jnp.bfloat16),
            pltpu.VMEM((e_count, total, LANES), jnp.float32),
            pltpu.VMEM((total, f), jnp.float32),
            pltpu.VMEM((total, f), jnp.float32),
            pltpu.VMEM((e_count, total, f), jnp.bfloat16),
            pltpu.VMEM((slots, side_len, side_len), jnp.bfloat16),
            pltpu.SemaphoreType.DMA((slots,)),
        ],
        compiler_params=pltpu.CompilerParams(vmem_limit_bytes=-(-scratch // MIB) * MIB),
        cost_estimate=pl.CostEstimate(
            flops=6 * total * d * f * e_count, bytes_accessed=4 * d * f * e_count, transcendentals=0
        ),
    )(*[pltpu.with_memory_space_constraint(w, pltpu.HBM) for w in weights], token, *[in_vmem(x) for x in ins])

    sums = []
    for send, keep in zip(results[:2], results[2:]):
        s = keep + exchange(send, 0, 1).astype(jnp.float32)
        got = [
            exchange(s[i * rows : (i + 1) * rows].astype(jnp.bfloat16), *k)
            for i, k in enumerate(near_offsets(), 1)
        ]
        sums.append(s[:rows] + sum(g.astype(jnp.float32) for g in got))
    s = jnp.concatenate(sums, axis=1)
    got = [
        exchange(s[i * own : (i + 1) * own].astype(jnp.bfloat16), *k)
        for i, k in enumerate(far_offsets(), 1)
    ]
    s = s[:own] + sum(g.astype(jnp.float32) for g in got)
    return s.astype(jnp.bfloat16)


def solution(mesh):
    in_specs = (
        P(("expert", "tensor"), None),
        P(("expert", "tensor"), None),
        P(("expert", "tensor"), None),
        P("expert", None, "tensor"),
        P("expert", None, "tensor"),
        P("expert", "tensor", None),
    )
    out_specs = P(("expert", "tensor"), None)
    return jax.shard_map(shards, mesh=mesh, in_specs=in_specs, out_specs=out_specs, check_vma=False)
```

```python
import functools
import jax
import jax.numpy as jnp
from jax import lax
from jax.experimental import pallas as pl
from jax.experimental.pallas import tpu as pltpu
from jax.sharding import PartitionSpec as P

LANES = 128
BOTH = ("expert", "tensor")
VMEM = pl.BlockSpec(memory_space=pltpu.VMEM)
HBM = pl.BlockSpec(memory_space=pltpu.HBM)
MIB = 1 << 20
SIDES = 2


def exchange(x, ke, kt):
    ne, nt = lax.axis_size("expert"), lax.axis_size("tensor")
    pairs = [(e * nt + t, (e ^ ke) * nt + (t ^ kt)) for e in range(ne) for t in range(nt)]
    return lax.ppermute(x, BOTH, pairs)


def near_offsets():
    return [(e, y) for e in range(lax.axis_size("expert")) for y in (0, 2)][1:]


def far_offsets():
    return [(0, 4 * k) for k in range(1, lax.axis_size("tensor") // 4)]


def in_vmem(x):
    return pltpu.with_memory_space_constraint(x, pltpu.VMEM)


def unit_of(ref, spot):
    kind, e, half, h = spot
    return ref.at[e, :, pl.ds(half * h, h)] if kind == 2 else ref.at[e, pl.ds(half * h, h), :]


def stage(compute, weights, loads, deps, ins, outs, scratch, flops, limit):
    n_load, n_in = len(loads), len(ins)
    kinds = sorted({spot[0] for spot in loads})
    used = [weights[k] for k in kinds]
    e_count, d, f = weights[0].shape
    shapes = [(f, spot[3]) if spot[0] == 2 else (spot[3], f) for spot in loads]

    def kernel(*refs):
        refs = list(refs)
        hbm = {k: refs.pop(0) for k in kinds}
        del refs[: len(deps)]
        in_refs = [refs.pop(0) for _ in range(n_in)]
        unit_refs = [refs.pop(0) for _ in range(n_load)]
        token_ref = refs.pop(0)
        out_refs = [refs.pop(0) for _ in outs]
        sems = refs.pop() if n_load else None
        copies = [
            pltpu.make_async_copy(unit_of(hbm[spot[0]], spot), unit_refs[i], sems.at[i])
            for i, spot in enumerate(loads)
        ]
        for copy in copies:
            copy.start()
        token_ref[...] = jnp.zeros_like(token_ref)
        if compute is not None:
            compute(in_refs, out_refs, refs)
        for copy in copies:
            copy.wait()

    size = sum(2 * a * b for a, b in shapes)
    results = pl.pallas_call(
        kernel,
        in_specs=[HBM] * len(used) + [pl.BlockSpec(memory_space=pl.ANY)] * len(deps) + [VMEM] * n_in,
        out_specs=[VMEM] * (n_load + 1 + len(outs)),
        out_shape=[pltpu.VMEM(s, jnp.bfloat16) for s in shapes]
        + [pltpu.VMEM((8, LANES), jnp.float32)]
        + [pltpu.VMEM(s, t) for s, t in outs],
        scratch_shapes=list(scratch) + ([pltpu.SemaphoreType.DMA((n_load,))] if n_load else []),
        compiler_params=pltpu.CompilerParams(vmem_limit_bytes=limit),
        cost_estimate=pl.CostEstimate(flops=flops, bytes_accessed=size, transcendentals=0),
    )(*[pltpu.with_memory_space_constraint(w, pltpu.HBM) for w in used], *deps, *[in_vmem(x) for x in ins])
    return list(results[:n_load]), results[n_load], list(results[n_load + 1 :])


def columns(count, step, body):
    for i in range(0, count, step):
        body(slice(i, i + step))


def dot(a, b):
    return jnp.dot(a, b, preferred_element_type=jnp.float32)


def shards(tokens, gate_weights, expert_ids, w_gate, w_up, w_down):
    weights = (w_gate, w_up, w_down)
    e_count, d, f = w_gate.shape
    ne, nt = lax.axis_size("expert"), lax.axis_size("tensor")
    own = tokens.shape[0]
    total = own * ne * nt
    half = d // 2
    fb = min(256, f)
    rows = own * (nt // 4)

    top = expert_ids.shape[1]

    def pack(gates_hbm, ids_hbm, tokens_hbm, out_ref, gates_ref, ids_ref, sems):
        copies = [
            pltpu.make_async_copy(gates_hbm, gates_ref, sems.at[0]),
            pltpu.make_async_copy(ids_hbm, ids_ref, sems.at[1]),
            pltpu.make_async_copy(tokens_hbm, out_ref.at[:, pl.ds(LANES, d)], sems.at[2]),
        ]
        for copy in copies:
            copy.start()
        row = lax.broadcasted_iota(jnp.int32, (own, own), 0)
        diagonal = row == lax.broadcasted_iota(jnp.int32, (own, own), 1)
        lane = lax.broadcasted_iota(jnp.int32, (own, LANES), 1)
        meta = jnp.zeros((own, LANES), jnp.float32)
        for n, ref in enumerate((gates_ref, ids_ref)):
            copies[n].wait()
            for i in range(top):
                line = ref[i : i + 1, :].astype(jnp.float32)
                col = jnp.sum(jnp.where(diagonal, line, 0.0), axis=1, keepdims=True)
                meta = jnp.where(lane == n * top + i, col, meta)
        out_ref[:, :LANES] = meta.astype(jnp.bfloat16)
        copies[2].wait()

    packed = pl.pallas_call(
        pack,
        in_specs=[HBM] * 3,
        out_specs=VMEM,
        out_shape=pltpu.VMEM((own, LANES + d), jnp.bfloat16),
        scratch_shapes=[
            pltpu.VMEM((top, own), gate_weights.dtype),
            pltpu.VMEM((top, own), expert_ids.dtype),
            pltpu.SemaphoreType.DMA((3,)),
        ],
        compiler_params=pltpu.CompilerParams(vmem_limit_bytes=MIB),
    )(*[pltpu.with_memory_space_constraint(x, pltpu.HBM) for x in (gate_weights.T, expert_ids.T, tokens)])

    def load_only(loads, *deps):
        units, token, _ = stage(None, weights, loads, deps, [], [], [], 0, 2 * MIB)
        return units, token

    last = e_count - 1
    resident = [(k, last, 0, half) for k in (0, 1)]
    resident += [(k, e, h, half) for e in range(last) for k in (0, 1) for h in (0, 1)]
    cut = len(resident) // 2
    far = [exchange(packed, *k) for k in far_offsets()]
    units, token = load_only(resident[:cut], packed)
    block = jnp.concatenate([packed] + far, axis=0)
    block, token = lax.optimization_barrier((block, token))
    pieces = [block] + [exchange(block, *k) for k in near_offsets()]
    more, token = load_only(resident[cut:], block, token)
    pieces[-1], token = lax.optimization_barrier((pieces[-1], token))
    units = units + more
    pieces = pieces + [exchange(p, 0, 1) for p in pieces]

    chunk = 1024
    n_d = d // chunk
    down = [(e, j) for j in range(n_d) for e in range(e_count)]
    per_unit = half // chunk
    spares = len(down) // per_unit if f == chunk and len(down) <= 4 * per_unit else 0

    def kernel(*refs):
        refs = list(refs)
        wg, wu, wd = refs[:3]
        del refs[:4]
        xrefs = [refs.pop(0) for _ in pieces]
        held = {spot[:3]: refs.pop(0) for spot in resident}
        sends = [refs.pop(0) for _ in range(SIDES)]
        keeps = [refs.pop(0) for _ in range(SIDES)]
        spare = [refs.pop(0) for _ in range(spares)]
        xs, gate_ref, h_ref, tail, landing, sems = refs

        def slot(i):
            return spare[i // per_unit].at[pl.ds(i % per_unit * chunk, chunk), :] if spares else landing.at[i]

        tails = [
            pltpu.make_async_copy(w.at[last, pl.ds(half, half), :], tail.at[k], sems.at[k])
            for k, w in enumerate((wg, wu))
        ]
        downs = [
            pltpu.make_async_copy(wd.at[e, :, pl.ds(j * chunk, chunk)], slot(i), sems.at[2 + i])
            for i, (e, j) in enumerate(down)
        ]
        for copy in tails:
            copy.start()
        me = lax.axis_index("expert")
        for i, ref in enumerate(xrefs):
            r = slice(i * rows, (i + 1) * rows)
            xs[r, :] = ref[:, LANES:]
            meta = ref[:, :LANES].astype(jnp.float32)
            for e in range(e_count):
                expert = (me * e_count + e).astype(jnp.float32)
                col = sum(
                    jnp.where(meta[:, top + i : top + i + 1] == expert, meta[:, i : i + 1], 0.0)
                    for i in range(top)
                )
                gate_ref[e, r, :] = jnp.broadcast_to(col, meta.shape)

        for e in range(e_count):
            def part(k, h):
                return tail.at[k] if e == last and h else held[k, e, h]

            if e == last:
                for copy in tails:
                    copy.wait()

            def hide(c):
                g = dot(xs[:, :half], part(0, 0)[:, c]) + dot(xs[:, half:], part(0, 1)[:, c])
                u = dot(xs[:, :half], part(1, 0)[:, c]) + dot(xs[:, half:], part(1, 1)[:, c])
                h_ref[e, :, c] = (g / (1.0 + jnp.exp(-g)) * u).astype(jnp.bfloat16)

            if e < last:

                @pl.when(me >= 0)
                def _():
                    columns(f, fb, hide)
            else:
                columns(f, fb, hide)

            if e == 0:
                for copy in downs:
                    copy.start()
        for j in range(n_d):
            at = range(j * e_count, (j + 1) * e_count)
            views = [slot(i) for i in at]
            for i in at:
                downs[i].wait()
            side, start = divmod(j * chunk, d // SIDES)

            def out(c):
                s = sum(dot(h_ref[e], views[e][:, c]) * gate_ref[e, :, 0:1] for e in range(e_count))
                to = slice(c.start + start, c.stop + start)
                keeps[side][:, to] = s[: total // 2]
                sends[side][:, to] = s[total // 2 :].astype(jnp.bfloat16)

            columns(chunk, 256, out)

    landing = (1, 16, LANES) if spares else (len(down), f, chunk)
    scratch = 2048 * total + 2 * total * d + 4 * e_count * total * LANES + 2 * e_count * total * f
    scratch += 4 * half * f + 2 * landing[0] * landing[1] * landing[2]
    ins = pieces + units
    results = pl.pallas_call(
        kernel,
        in_specs=[HBM] * 3 + [pl.BlockSpec(memory_space=pl.ANY)] + [VMEM] * len(ins),
        out_specs=[VMEM] * (2 * SIDES + spares),
        out_shape=[pltpu.VMEM((total // 2, d // SIDES), jnp.bfloat16)] * SIDES
        + [pltpu.VMEM((total // 2, d // SIDES), jnp.float32)] * SIDES
        + [pltpu.VMEM((half, f), jnp.bfloat16)] * spares,
        input_output_aliases={4 + len(pieces) + 2 + i: 2 * SIDES + i for i in range(spares)},
        scratch_shapes=[
            pltpu.VMEM((total, d), jnp.bfloat16),
            pltpu.VMEM((e_count, total, LANES), jnp.float32),
            pltpu.VMEM((e_count, total, f), jnp.bfloat16),
            pltpu.VMEM((2, half, f), jnp.bfloat16),
            pltpu.VMEM(landing, jnp.bfloat16),
            pltpu.SemaphoreType.DMA((2 + len(down),)),
        ],
        compiler_params=pltpu.CompilerParams(vmem_limit_bytes=-(-scratch // MIB) * MIB),
        cost_estimate=pl.CostEstimate(
            flops=6 * total * d * f * e_count, bytes_accessed=4 * d * f * e_count, transcendentals=0
        ),
    )(*[pltpu.with_memory_space_constraint(w, pltpu.HBM) for w in weights], token, *[in_vmem(x) for x in ins])

    sums = []
    for send, keep in zip(results[:SIDES], results[SIDES : 2 * SIDES]):
        s = keep + exchange(send, 0, 1).astype(jnp.float32)
        got = [
            exchange(s[i * rows : (i + 1) * rows].astype(jnp.bfloat16), *k)
            for i, k in enumerate(near_offsets(), 1)
        ]
        sums.append(s[:rows] + sum(g.astype(jnp.float32) for g in got))
    s = jnp.concatenate(sums, axis=1)
    got = [
        exchange(s[i * own : (i + 1) * own].astype(jnp.bfloat16), *k)
        for i, k in enumerate(far_offsets(), 1)
    ]
    s = s[:own] + sum(g.astype(jnp.float32) for g in got)
    return s.astype(jnp.bfloat16)


def solution(mesh):
    in_specs = (
        P(("expert", "tensor"), None),
        P(("expert", "tensor"), None),
        P(("expert", "tensor"), None),
        P("expert", None, "tensor"),
        P("expert", None, "tensor"),
        P("expert", "tensor", None),
    )
    out_specs = P(("expert", "tensor"), None)
    return jax.shard_map(shards, mesh=mesh, in_specs=in_specs, out_specs=out_specs, check_vma=False)
```

```python
import functools
import jax
import jax.numpy as jnp
from jax import lax
from jax.experimental import pallas as pl
from jax.experimental.pallas import tpu as pltpu
from jax.sharding import PartitionSpec as P

LANES = 128
BOTH = ("expert", "tensor")
VMEM = pl.BlockSpec(memory_space=pltpu.VMEM)
HBM = pl.BlockSpec(memory_space=pltpu.HBM)
MIB = 1 << 20
SIDES = 2


def exchange(x, ke, kt):
    ne, nt = lax.axis_size("expert"), lax.axis_size("tensor")
    pairs = [(e * nt + t, (e ^ ke) * nt + (t ^ kt)) for e in range(ne) for t in range(nt)]
    return lax.ppermute(x, BOTH, pairs)


def near_offsets():
    return [(e, y) for e in range(lax.axis_size("expert")) for y in (0, 2)][1:]


def far_offsets():
    return [(0, 4 * k) for k in range(1, lax.axis_size("tensor") // 4)]


def in_vmem(x):
    return pltpu.with_memory_space_constraint(x, pltpu.VMEM)


def unit_of(ref, spot):
    kind, e, half, h = spot
    return ref.at[e, :, pl.ds(half * h, h)] if kind == 2 else ref.at[e, pl.ds(half * h, h), :]


def stage(compute, weights, loads, deps, ins, outs, scratch, flops, limit):
    n_load, n_in = len(loads), len(ins)
    kinds = sorted({spot[0] for spot in loads})
    used = [weights[k] for k in kinds]
    e_count, d, f = weights[0].shape
    shapes = [(f, spot[3]) if spot[0] == 2 else (spot[3], f) for spot in loads]

    def kernel(*refs):
        refs = list(refs)
        hbm = {k: refs.pop(0) for k in kinds}
        del refs[: len(deps)]
        in_refs = [refs.pop(0) for _ in range(n_in)]
        unit_refs = [refs.pop(0) for _ in range(n_load)]
        token_ref = refs.pop(0)
        out_refs = [refs.pop(0) for _ in outs]
        sems = refs.pop() if n_load else None
        copies = [
            pltpu.make_async_copy(unit_of(hbm[spot[0]], spot), unit_refs[i], sems.at[i])
            for i, spot in enumerate(loads)
        ]
        for copy in copies:
            copy.start()
        token_ref[...] = jnp.zeros_like(token_ref)
        if compute is not None:
            compute(in_refs, out_refs, refs)
        for copy in copies:
            copy.wait()

    size = sum(2 * a * b for a, b in shapes)
    results = pl.pallas_call(
        kernel,
        in_specs=[HBM] * len(used) + [pl.BlockSpec(memory_space=pl.ANY)] * len(deps) + [VMEM] * n_in,
        out_specs=[VMEM] * (n_load + 1 + len(outs)),
        out_shape=[pltpu.VMEM(s, jnp.bfloat16) for s in shapes]
        + [pltpu.VMEM((8, LANES), jnp.float32)]
        + [pltpu.VMEM(s, t) for s, t in outs],
        scratch_shapes=list(scratch) + ([pltpu.SemaphoreType.DMA((n_load,))] if n_load else []),
        compiler_params=pltpu.CompilerParams(vmem_limit_bytes=limit),
        cost_estimate=pl.CostEstimate(flops=flops, bytes_accessed=size, transcendentals=0),
    )(*[pltpu.with_memory_space_constraint(w, pltpu.HBM) for w in used], *deps, *[in_vmem(x) for x in ins])
    return list(results[:n_load]), results[n_load], list(results[n_load + 1 :])


def columns(count, step, body):
    for i in range(0, count, step):
        body(slice(i, i + step))


def dot(a, b):
    return jnp.dot(a, b, preferred_element_type=jnp.float32)


def shards(tokens, gate_weights, expert_ids, w_gate, w_up, w_down):
    weights = (w_gate, w_up, w_down)
    e_count, d, f = w_gate.shape
    ne, nt = lax.axis_size("expert"), lax.axis_size("tensor")
    own = tokens.shape[0]
    total = own * ne * nt
    half = d // 2
    fb = min(256, f)
    rows = own * (nt // 4)

    top = expert_ids.shape[1]

    def pack(gates_hbm, ids_hbm, tokens_hbm, out_ref, gates_ref, ids_ref, sems):
        copies = [
            pltpu.make_async_copy(gates_hbm, gates_ref, sems.at[0]),
            pltpu.make_async_copy(ids_hbm, ids_ref, sems.at[1]),
            pltpu.make_async_copy(tokens_hbm, out_ref.at[:, pl.ds(LANES, d)], sems.at[2]),
        ]
        for copy in copies:
            copy.start()
        row = lax.broadcasted_iota(jnp.int32, (own, own), 0)
        diagonal = row == lax.broadcasted_iota(jnp.int32, (own, own), 1)
        lane = lax.broadcasted_iota(jnp.int32, (own, LANES), 1)
        meta = jnp.zeros((own, LANES), jnp.float32)
        for n, ref in enumerate((gates_ref, ids_ref)):
            copies[n].wait()
            for i in range(top):
                line = ref[i : i + 1, :].astype(jnp.float32)
                col = jnp.sum(jnp.where(diagonal, line, 0.0), axis=1, keepdims=True)
                meta = jnp.where(lane == n * top + i, col, meta)
        out_ref[:, :LANES] = meta.astype(jnp.bfloat16)
        copies[2].wait()

    packed = pl.pallas_call(
        pack,
        in_specs=[HBM] * 3,
        out_specs=VMEM,
        out_shape=pltpu.VMEM((own, LANES + d), jnp.bfloat16),
        scratch_shapes=[
            pltpu.VMEM((top, own), gate_weights.dtype),
            pltpu.VMEM((top, own), expert_ids.dtype),
            pltpu.SemaphoreType.DMA((3,)),
        ],
        compiler_params=pltpu.CompilerParams(vmem_limit_bytes=MIB),
    )(*[pltpu.with_memory_space_constraint(x, pltpu.HBM) for x in (gate_weights.T, expert_ids.T, tokens)])

    def load_only(loads, *deps):
        units, token, _ = stage(None, weights, loads, deps, [], [], [], 0, 2 * MIB)
        return units, token

    last = e_count - 1
    resident = [(k, last, 0, half) for k in (0, 1)]
    resident += [(k, e, h, half) for e in range(last) for k in (0, 1) for h in (0, 1)]
    cut = 2
    far = [exchange(packed, *k) for k in far_offsets()]
    units, token = load_only(resident[:cut], packed)
    block = jnp.concatenate([packed] + far, axis=0)
    block, token = lax.optimization_barrier((block, token))
    pieces = [block] + [exchange(block, *k) for k in near_offsets()]
    more, token = load_only(resident[cut:5], block, token)
    units = units + more
    more, token = load_only(resident[5:], block, token)
    pieces[-1], token = lax.optimization_barrier((pieces[-1], token))
    units = units + more
    pieces = pieces + [exchange(p, 0, 1) for p in pieces]

    chunk = 1024
    n_d = d // chunk
    down = [(e, j) for j in range(n_d) for e in range(e_count)]
    per_unit = half // chunk
    spares = len(down) // per_unit if f == chunk and len(down) <= 4 * per_unit else 0

    def kernel(*refs):
        refs = list(refs)
        wg, wu, wd = refs[:3]
        del refs[:4]
        xrefs = [refs.pop(0) for _ in pieces]
        held = {spot[:3]: refs.pop(0) for spot in resident}
        sends = [refs.pop(0) for _ in range(SIDES)]
        keeps = [refs.pop(0) for _ in range(SIDES)]
        spare = [refs.pop(0) for _ in range(spares)]
        xs, gate_ref, h_ref, tail, landing, sems = refs

        def slot(i):
            return spare[i // per_unit].at[pl.ds(i % per_unit * chunk, chunk), :] if spares else landing.at[i]

        tails = [
            pltpu.make_async_copy(w.at[last, pl.ds(half, half), :], tail.at[k], sems.at[k])
            for k, w in enumerate((wg, wu))
        ]
        downs = [
            pltpu.make_async_copy(wd.at[e, :, pl.ds(j * chunk, chunk)], slot(i), sems.at[2 + i])
            for i, (e, j) in enumerate(down)
        ]
        for copy in tails:
            copy.start()
        me = lax.axis_index("expert")
        for i, ref in enumerate(xrefs):
            r = slice(i * rows, (i + 1) * rows)
            xs[r, :] = ref[:, LANES:]
            meta = ref[:, :LANES].astype(jnp.float32)
            for e in range(e_count):
                expert = (me * e_count + e).astype(jnp.float32)
                col = sum(
                    jnp.where(meta[:, top + i : top + i + 1] == expert, meta[:, i : i + 1], 0.0)
                    for i in range(top)
                )
                gate_ref[e, r, :] = jnp.broadcast_to(col, meta.shape)

        for e in range(e_count):
            def part(k, h):
                return tail.at[k] if e == last and h else held[k, e, h]

            if e == last:
                for copy in tails:
                    copy.wait()

            def hide(c):
                g = dot(xs[:, :half], part(0, 0)[:, c]) + dot(xs[:, half:], part(0, 1)[:, c])
                u = dot(xs[:, :half], part(1, 0)[:, c]) + dot(xs[:, half:], part(1, 1)[:, c])
                h_ref[e, :, c] = (g / (1.0 + jnp.exp(-g)) * u).astype(jnp.bfloat16)

            if e < last:

                @pl.when(me >= 0)
                def _():
                    columns(f, fb, hide)
            else:
                columns(f, fb, hide)

            if e == 0:
                for copy in downs:
                    copy.start()
        for j in range(n_d):
            at = range(j * e_count, (j + 1) * e_count)
            views = [slot(i) for i in at]
            for i in at:
                downs[i].wait()
            side, start = divmod(j * chunk, d // SIDES)

            def out(c):
                s = sum(dot(h_ref[e], views[e][:, c]) * gate_ref[e, :, 0:1] for e in range(e_count))
                to = slice(c.start + start, c.stop + start)
                keeps[side][:, to] = s[: total // 2]
                sends[side][:, to] = s[total // 2 :].astype(jnp.bfloat16)

            columns(chunk, 256, out)

    landing = (1, 16, LANES) if spares else (len(down), f, chunk)
    scratch = 2048 * total + 2 * total * d + 4 * e_count * total * LANES + 2 * e_count * total * f
    scratch += 4 * half * f + 2 * landing[0] * landing[1] * landing[2]
    ins = pieces + units
    results = pl.pallas_call(
        kernel,
        in_specs=[HBM] * 3 + [pl.BlockSpec(memory_space=pl.ANY)] + [VMEM] * len(ins),
        out_specs=[VMEM] * (2 * SIDES + spares),
        out_shape=[pltpu.VMEM((total // 2, d // SIDES), jnp.bfloat16)] * SIDES
        + [pltpu.VMEM((total // 2, d // SIDES), jnp.float32)] * SIDES
        + [pltpu.VMEM((half, f), jnp.bfloat16)] * spares,
        input_output_aliases={4 + len(pieces) + 2 + i: 2 * SIDES + i for i in range(spares)},
        scratch_shapes=[
            pltpu.VMEM((total, d), jnp.bfloat16),
            pltpu.VMEM((e_count, total, LANES), jnp.float32),
            pltpu.VMEM((e_count, total, f), jnp.bfloat16),
            pltpu.VMEM((2, half, f), jnp.bfloat16),
            pltpu.VMEM(landing, jnp.bfloat16),
            pltpu.SemaphoreType.DMA((2 + len(down),)),
        ],
        compiler_params=pltpu.CompilerParams(vmem_limit_bytes=-(-scratch // MIB) * MIB),
        cost_estimate=pl.CostEstimate(
            flops=6 * total * d * f * e_count, bytes_accessed=4 * d * f * e_count, transcendentals=0
        ),
    )(*[pltpu.with_memory_space_constraint(w, pltpu.HBM) for w in weights], token, *[in_vmem(x) for x in ins])

    sums = []
    for send, keep in zip(results[:SIDES], results[SIDES : 2 * SIDES]):
        s = keep + exchange(send, 0, 1).astype(jnp.float32)
        got = [
            exchange(s[i * rows : (i + 1) * rows].astype(jnp.bfloat16), *k)
            for i, k in enumerate(near_offsets(), 1)
        ]
        sums.append(s[:rows] + sum(g.astype(jnp.float32) for g in got))
    s = jnp.concatenate(sums, axis=1)
    got = [
        exchange(s[i * own : (i + 1) * own].astype(jnp.bfloat16), *k)
        for i, k in enumerate(far_offsets(), 1)
    ]
    s = s[:own] + sum(g.astype(jnp.float32) for g in got)
    return s.astype(jnp.bfloat16)


def solution(mesh):
    in_specs = (
        P(("expert", "tensor"), None),
        P(("expert", "tensor"), None),
        P(("expert", "tensor"), None),
        P("expert", None, "tensor"),
        P("expert", None, "tensor"),
        P("expert", "tensor", None),
    )
    out_specs = P(("expert", "tensor"), None)
    return jax.shard_map(shards, mesh=mesh, in_specs=in_specs, out_specs=out_specs, check_vma=False)
```

```python
import functools
import jax
import jax.numpy as jnp
from jax import lax
from jax.experimental import pallas as pl
from jax.experimental.pallas import tpu as pltpu
from jax.sharding import PartitionSpec as P

LANES = 128
BOTH = ("expert", "tensor")
VMEM = pl.BlockSpec(memory_space=pltpu.VMEM)
HBM = pl.BlockSpec(memory_space=pltpu.HBM)
MIB = 1 << 20
SIDES = 2


def exchange(x, ke, kt):
    ne, nt = lax.axis_size("expert"), lax.axis_size("tensor")
    pairs = [(e * nt + t, (e ^ ke) * nt + (t ^ kt)) for e in range(ne) for t in range(nt)]
    return lax.ppermute(x, BOTH, pairs)


def near_offsets():
    return [(e, y) for e in range(lax.axis_size("expert")) for y in (0, 2)][:0:-1]


def far_offsets():
    return [(0, 4 * k) for k in range(lax.axis_size("tensor") // 4 - 1, 0, -1)]


def in_vmem(x):
    return pltpu.with_memory_space_constraint(x, pltpu.VMEM)


def unit_of(ref, spot):
    kind, e, half, h = spot
    return ref.at[e, :, pl.ds(half * h, h)] if kind == 2 else ref.at[e, pl.ds(half * h, h), :]


def stage(compute, weights, loads, deps, ins, outs, scratch, flops, limit):
    n_load, n_in = len(loads), len(ins)
    kinds = sorted({spot[0] for spot in loads})
    used = [weights[k] for k in kinds]
    e_count, d, f = weights[0].shape
    shapes = [(f, spot[3]) if spot[0] == 2 else (spot[3], f) for spot in loads]

    def kernel(*refs):
        refs = list(refs)
        hbm = {k: refs.pop(0) for k in kinds}
        del refs[: len(deps)]
        in_refs = [refs.pop(0) for _ in range(n_in)]
        unit_refs = [refs.pop(0) for _ in range(n_load)]
        token_ref = refs.pop(0)
        out_refs = [refs.pop(0) for _ in outs]
        sems = refs.pop() if n_load else None
        copies = [
            pltpu.make_async_copy(unit_of(hbm[spot[0]], spot), unit_refs[i], sems.at[i])
            for i, spot in enumerate(loads)
        ]
        for copy in copies:
            copy.start()
        token_ref[...] = jnp.zeros_like(token_ref)
        if compute is not None:
            compute(in_refs, out_refs, refs)
        for copy in copies:
            copy.wait()

    size = sum(2 * a * b for a, b in shapes)
    results = pl.pallas_call(
        kernel,
        in_specs=[HBM] * len(used) + [pl.BlockSpec(memory_space=pl.ANY)] * len(deps) + [VMEM] * n_in,
        out_specs=[VMEM] * (n_load + 1 + len(outs)),
        out_shape=[pltpu.VMEM(s, jnp.bfloat16) for s in shapes]
        + [pltpu.VMEM((8, LANES), jnp.float32)]
        + [pltpu.VMEM(s, t) for s, t in outs],
        scratch_shapes=list(scratch) + ([pltpu.SemaphoreType.DMA((n_load,))] if n_load else []),
        compiler_params=pltpu.CompilerParams(vmem_limit_bytes=limit),
        cost_estimate=pl.CostEstimate(flops=flops, bytes_accessed=size, transcendentals=0),
    )(*[pltpu.with_memory_space_constraint(w, pltpu.HBM) for w in used], *deps, *[in_vmem(x) for x in ins])
    return list(results[:n_load]), results[n_load], list(results[n_load + 1 :])


def columns(count, step, body):
    for i in range(0, count, step):
        body(slice(i, i + step))


def dot(a, b):
    return jnp.dot(a, b, preferred_element_type=jnp.float32)


def shards(tokens, gate_weights, expert_ids, w_gate, w_up, w_down):
    weights = (w_gate, w_up, w_down)
    e_count, d, f = w_gate.shape
    ne, nt = lax.axis_size("expert"), lax.axis_size("tensor")
    own = tokens.shape[0]
    total = own * ne * nt
    half = d // 2
    fb = min(256, f)
    rows = own * (nt // 4)

    top = expert_ids.shape[1]

    def pack(gates_hbm, ids_hbm, tokens_hbm, out_ref, gates_ref, ids_ref, sems):
        copies = [
            pltpu.make_async_copy(gates_hbm, gates_ref, sems.at[0]),
            pltpu.make_async_copy(ids_hbm, ids_ref, sems.at[1]),
            pltpu.make_async_copy(tokens_hbm, out_ref.at[:, pl.ds(LANES, d)], sems.at[2]),
        ]
        for copy in copies:
            copy.start()
        row = lax.broadcasted_iota(jnp.int32, (own, own), 0)
        diagonal = row == lax.broadcasted_iota(jnp.int32, (own, own), 1)
        lane = lax.broadcasted_iota(jnp.int32, (own, LANES), 1)
        meta = jnp.zeros((own, LANES), jnp.float32)
        for n, ref in enumerate((gates_ref, ids_ref)):
            copies[n].wait()
            for i in range(top):
                line = ref[i : i + 1, :].astype(jnp.float32)
                col = jnp.sum(jnp.where(diagonal, line, 0.0), axis=1, keepdims=True)
                meta = jnp.where(lane == n * top + i, col, meta)
        out_ref[:, :LANES] = meta.astype(jnp.bfloat16)
        copies[2].wait()

    packed = pl.pallas_call(
        pack,
        in_specs=[HBM] * 3,
        out_specs=VMEM,
        out_shape=pltpu.VMEM((own, LANES + d), jnp.bfloat16),
        scratch_shapes=[
            pltpu.VMEM((top, own), gate_weights.dtype),
            pltpu.VMEM((top, own), expert_ids.dtype),
            pltpu.SemaphoreType.DMA((3,)),
        ],
        compiler_params=pltpu.CompilerParams(vmem_limit_bytes=MIB),
    )(*[pltpu.with_memory_space_constraint(x, pltpu.HBM) for x in (gate_weights.T, expert_ids.T, tokens)])

    def load_only(loads, *deps):
        units, token, _ = stage(None, weights, loads, deps, [], [], [], 0, 2 * MIB)
        return units, token

    last = e_count - 1
    resident = [(k, last, 0, half) for k in (0, 1)]
    resident += [(k, e, h, half) for e in range(last) for k in (0, 1) for h in (0, 1)]
    cut = 2
    far = [exchange(packed, *k) for k in far_offsets()]
    units, token = load_only(resident[:cut], packed)
    block = jnp.concatenate([packed] + far, axis=0)
    block, token = lax.optimization_barrier((block, token))
    pieces = [block] + [exchange(block, *k) for k in near_offsets()]
    more, token = load_only(resident[cut:5], block, token)
    units = units + more
    more, token = load_only(resident[5:], block, token)
    pieces[-1], token = lax.optimization_barrier((pieces[-1], token))
    units = units + more
    pieces = pieces + [exchange(p, 0, 1) for p in pieces]

    chunk = 1024
    n_d = d // chunk
    down = [(e, j) for j in range(n_d) for e in range(e_count)]
    per_unit = half // chunk
    spares = len(down) // per_unit if f == chunk and len(down) <= 4 * per_unit else 0

    def kernel(*refs):
        refs = list(refs)
        wg, wu, wd = refs[:3]
        del refs[:4]
        xrefs = [refs.pop(0) for _ in pieces]
        held = {spot[:3]: refs.pop(0) for spot in resident}
        sends = [refs.pop(0) for _ in range(SIDES)]
        keeps = [refs.pop(0) for _ in range(SIDES)]
        spare = [refs.pop(0) for _ in range(spares)]
        xs, gate_ref, h_ref, tail, landing, sems = refs

        def slot(i):
            return spare[i // per_unit].at[pl.ds(i % per_unit * chunk, chunk), :] if spares else landing.at[i]

        tails = [
            pltpu.make_async_copy(w.at[last, pl.ds(half, half), :], tail.at[k], sems.at[k])
            for k, w in enumerate((wg, wu))
        ]
        downs = [
            pltpu.make_async_copy(wd.at[e, :, pl.ds(j * chunk, chunk)], slot(i), sems.at[2 + i])
            for i, (e, j) in enumerate(down)
        ]
        for copy in tails:
            copy.start()
        me = lax.axis_index("expert")

        def fill():
            for i, ref in enumerate(xrefs):
                xs[i * rows : (i + 1) * rows, :] = ref[:, LANES:]

        def weigh():
            for i, ref in enumerate(xrefs):
                r = slice(i * rows, (i + 1) * rows)
                meta = ref[:, :LANES].astype(jnp.float32)
                for e in range(e_count):
                    expert = (me * e_count + e).astype(jnp.float32)
                    col = sum(
                        jnp.where(meta[:, top + i : top + i + 1] == expert, meta[:, i : i + 1], 0.0)
                        for i in range(top)
                    )
                    gate_ref[e, r, :] = jnp.broadcast_to(col, meta.shape)

        for e in range(e_count):
            def part(k, h):
                return tail.at[k] if e == last and h else held[k, e, h]

            if e == last:
                for copy in tails:
                    copy.wait()

            def hide(c):
                g = dot(xs[:, :half], part(0, 0)[:, c]) + dot(xs[:, half:], part(0, 1)[:, c])
                u = dot(xs[:, :half], part(1, 0)[:, c]) + dot(xs[:, half:], part(1, 1)[:, c])
                h_ref[e, :, c] = (g / (1.0 + jnp.exp(-g)) * u).astype(jnp.bfloat16)

            if e == 0:

                @pl.when(me >= 0)
                def _():
                    fill()
                    columns(f, fb, hide)
            else:
                if e == last:
                    weigh()
                columns(f, fb, hide)
            if e == 0:
                for copy in downs:
                    copy.start()
        for j in range(n_d):
            at = range(j * e_count, (j + 1) * e_count)
            views = [slot(i) for i in at]
            for i in at:
                downs[i].wait()
            side, start = divmod(j * chunk, d // SIDES)

            def out(c):
                s = sum(dot(h_ref[e], views[e][:, c]) * jnp.concatenate([gate_ref[e]] * (256 // LANES), axis=1) for e in range(e_count))
                to = slice(c.start + start, c.stop + start)
                keeps[side][:, to] = s[: total // 2]
                sends[side][:, to] = s[total // 2 :].astype(jnp.bfloat16)

            columns(chunk, 256, out)

    landing = (1, 16, LANES) if spares else (len(down), f, chunk)
    scratch = 2048 * total + 2 * total * d + 4 * e_count * total * LANES + 2 * e_count * total * f
    scratch += 4 * half * f + 2 * landing[0] * landing[1] * landing[2]
    ins = pieces + units
    results = pl.pallas_call(
        kernel,
        in_specs=[HBM] * 3 + [pl.BlockSpec(memory_space=pl.ANY)] + [VMEM] * len(ins),
        out_specs=[VMEM] * (2 * SIDES + spares),
        out_shape=[pltpu.VMEM((total // 2, d // SIDES), jnp.bfloat16)] * SIDES
        + [pltpu.VMEM((total // 2, d // SIDES), jnp.float32)] * SIDES
        + [pltpu.VMEM((half, f), jnp.bfloat16)] * spares,
        input_output_aliases={4 + len(pieces) + 2 + i: 2 * SIDES + i for i in range(spares)},
        scratch_shapes=[
            pltpu.VMEM((total, d), jnp.bfloat16),
            pltpu.VMEM((e_count, total, LANES), jnp.float32),
            pltpu.VMEM((e_count, total, f), jnp.bfloat16),
            pltpu.VMEM((2, half, f), jnp.bfloat16),
            pltpu.VMEM(landing, jnp.bfloat16),
            pltpu.SemaphoreType.DMA((2 + len(down),)),
        ],
        compiler_params=pltpu.CompilerParams(vmem_limit_bytes=-(-scratch // MIB) * MIB),
        cost_estimate=pl.CostEstimate(
            flops=6 * total * d * f * e_count, bytes_accessed=4 * d * f * e_count, transcendentals=0
        ),
    )(*[pltpu.with_memory_space_constraint(w, pltpu.HBM) for w in weights], token, *[in_vmem(x) for x in ins])

    sums = []
    for send, keep in zip(results[:SIDES], results[SIDES : 2 * SIDES]):
        s = keep + exchange(send, 0, 1).astype(jnp.float32)
        got = [
            exchange(s[i * rows : (i + 1) * rows].astype(jnp.bfloat16), *k)
            for i, k in enumerate(near_offsets(), 1)
        ]
        sums.append(s[:rows] + sum(g.astype(jnp.float32) for g in got))
    s = jnp.concatenate(sums, axis=1)
    got = [
        exchange(s[i * own : (i + 1) * own].astype(jnp.bfloat16), *k)
        for i, k in enumerate(far_offsets(), 1)
    ]
    s = s[:own] + sum(g.astype(jnp.float32) for g in got)
    return s.astype(jnp.bfloat16)


def solution(mesh):
    in_specs = (
        P(("expert", "tensor"), None),
        P(("expert", "tensor"), None),
        P(("expert", "tensor"), None),
        P("expert", None, "tensor"),
        P("expert", None, "tensor"),
        P("expert", "tensor", None),
    )
    out_specs = P(("expert", "tensor"), None)
    return jax.shard_map(shards, mesh=mesh, in_specs=in_specs, out_specs=out_specs, check_vma=False)
```
